32 devices in a mesh: groups: 2 (over x), lines: 16 (over z, y, core).
Axes of the slice: x: 2, y: 2, z: 4, core: 2. Of those that a mesh axis runs over, the one named last changes fastest.
Arguments:
- base_flow: bfloat16 [32768, 1024], P('lines', 'groups'), parts along dimension 1, may hold values from -6 to 6
- lodf_blocks: bfloat16 [3072, 128, 128], P('lines'), may hold values from -0.1796875 to 0.1796875
- block_row: int32 [3072], P('lines'), may hold values from 0 to 15, as said below
- block_col: int32 [3072], P('lines'), may hold values from 0 to 15, as said below
- block_count: int32 [16], P('lines'), may hold values from 64 to 192, as said below
- outage: int32 [2048], P('lines'), may hold values from 0 to 2047
- rating: int32 [32768], P('lines'), may hold values from 50 to 299
- cost: float32 [32768], P('lines'), may hold values from 0.3 to 9
Outputs:
- post_flow: bfloat16 [32768, 1024], P('lines', 'groups'), parts along dimension 1
- penalty: float32 [1024], P('groups'), parts along dimension 0
The draws below stay inside these ranges and needn't reach their ends.
There are 2 independent parts, one for each index of `groups`. The reference program is written for one: setup_inputs(seed, part) draws one part's arguments, and reference() takes and returns one part's arrays. A program takes and returns all parts, laid end to end along the dimension named above; an argument that names none is the same for every part. Nothing has to cross between parts.
Inputs may be any that keep to these rules, and one draw needn't show every extreme that they name: Within one area the slots name distinct pairs of block_row and block_col, used slots and unused alike. `block_col`: the slot of area a names an area at most 6 steps from a along lines, counted with wrap around. `block_count`: slots of an area past its count are unused.
All inputs are finite; a program needn't handle non-finite values.
Results may differ from the reference program's by a relative error of at most 0.001.
Values may be sent and summed in bfloat16 or wider, within the bound.
A program may use at most 64 MiB of HBM per device.

```python
import jax
import jax.numpy as jnp
from jax import lax

BLOCK = 128
LINE_DEV = 2048
NB_DEV = 192
REACH = 6
SCEN = 512
LINES = 32768
OUTAGES = 2048
NBLK = 3072


def slot_pairs(key):
    areas = NBLK // NB_DEV
    spread = 2 * REACH + 1
    choices_all = LINE_DEV // BLOCK * spread

    def one_area(area):
        picked = jax.random.permutation(jax.random.fold_in(key, area), choices_all)[:NB_DEV]
        return picked.astype(jnp.int32)
    picked = jax.vmap(one_area)(jnp.arange(areas, dtype=jnp.int32))
    rows = picked // spread
    cols = (jnp.arange(areas, dtype=jnp.int32)[:, None] + picked % spread - REACH) % areas
    return (rows.reshape(NBLK).astype(jnp.int32), cols.reshape(NBLK).astype(jnp.int32))


def draw_block_row(key, part):
    rows, cols = slot_pairs(key)
    return rows


def draw_block_col(key, part):
    rows, cols = slot_pairs(key)
    return cols


def draw_block_count(key, part):
    key = jax.random.fold_in(key, 5)
    first, second = jax.random.split(key)
    areas = NBLK // NB_DEV
    counts = jax.random.randint(first, (areas,), NB_DEV // 3, NB_DEV + 1)
    fullest = jax.random.randint(second, (), 0, areas)
    return counts.at[fullest].set(NB_DEV).astype(jnp.int32)


def draw_cost(key, part):
    key = jax.random.fold_in(key, 7)
    ramp = 1.0 + 2.0 * jnp.arange(LINES, dtype=jnp.float32) / LINES
    factor = jnp.exp(jax.random.uniform(key, (LINES,), jnp.float32, jnp.log(0.5), jnp.log(2.0)))
    return (ramp * factor).astype(jnp.float32)


def touch_ends(drawn, stream_key, low, top_value):
    longest = drawn.shape.index(max(drawn.shape))
    spots = []
    for shift in (0, 1):
        where = [jax.random.randint(jax.random.fold_in(stream_key, axis), (), 0, length) for axis, length in enumerate(drawn.shape)]
        where[longest] = (where[longest] + shift) % drawn.shape[longest]
        spots.append(tuple(where))
    return drawn.at[spots[0]].set(low).at[spots[1]].set(top_value)


def levels(stream_key, shape, shards, least, high):
    level, own = 1.0, jax.random.fold_in(stream_key, 6)
    for axis_at, shards_of in shards:
        steps = jnp.exp(jax.random.uniform(jax.random.fold_in(own, axis_at), (shards_of,), jnp.float32, least / len(shards), high / len(shards)))
        level = level * jnp.repeat(steps, shape[axis_at] // shards_of).reshape([-1 if axis == axis_at else 1 for axis in range(len(shape))])
    return level


def centred(key, dims, width, reach, cuts=(), kind=jnp.bfloat16):
    result = jax.random.normal(key, dims, jnp.float32) * width
    if len(cuts) > 0:
        result = levels(key, dims, cuts, -0.22, 0.18) * result
    return jnp.clip(result, min=-reach, max=reach).astype(kind)


def setup_inputs(seed: int = 0, part: int = 0) -> dict:
    arg_keys = jax.random.split(jax.random.key(seed), 9)
    part_keys = jax.random.split(jax.random.fold_in(arg_keys[8], part), 9)
    return {
        "base_flow": centred(part_keys[0], (LINES, SCEN), 1.0, 6.0, ((0, 16),)),
        "lodf_blocks": centred(arg_keys[1], (NBLK, BLOCK, BLOCK), 0.03, 0.1796875, ((0, 16),)),
        "block_row": draw_block_row(jax.random.fold_in(arg_keys[8], 71), part),
        "block_col": draw_block_col(jax.random.fold_in(arg_keys[8], 71), part),
        "block_count": draw_block_count(jax.random.fold_in(arg_keys[8], 71), part),
        "outage": touch_ends(jax.random.randint(arg_keys[5], (OUTAGES,), 0, LINE_DEV), jax.random.fold_in(arg_keys[5], 1), 0, LINE_DEV - 1).astype(jnp.int32),
        "rating": touch_ends(jax.random.randint(arg_keys[6], (LINES,), 50, 300), jax.random.fold_in(arg_keys[6], 1), 50, 299).astype(jnp.int32),
        "cost": draw_cost(jax.random.fold_in(arg_keys[8], 71), part),
    }


def reference(base_flow, lodf_blocks, block_row, block_col, block_count, outage, rating, cost):
    areas = NBLK // NB_DEV
    rows_blocks = LINE_DEV // BLOCK
    shifted = outage + (jnp.arange(OUTAGES, dtype=jnp.int32) // BLOCK) * LINE_DEV
    panel = jnp.take(base_flow, shifted.astype(jnp.int32), axis=0).reshape(areas, BLOCK, SCEN)

    def one_area(carry, area):
        blocks = lax.dynamic_slice_in_dim(lodf_blocks, area * NB_DEV, NB_DEV, 0).astype(jnp.float32)
        rows = lax.dynamic_slice_in_dim(block_row, area * NB_DEV, NB_DEV, 0)
        cols = lax.dynamic_slice_in_dim(block_col, area * NB_DEV, NB_DEV, 0)
        count = lax.dynamic_slice_in_dim(block_count, area, 1, 0)[0]
        pieces = jnp.take(panel, cols, axis=0).astype(jnp.float32)
        terms = jnp.einsum("bij,bjs->bis", blocks, pieces, precision=lax.Precision.HIGHEST)
        used = (jnp.arange(NB_DEV, dtype=jnp.int32) < count).astype(jnp.float32)
        picker = (rows[None, :] == jnp.arange(rows_blocks, dtype=jnp.int32)[:, None]).astype(jnp.float32) * used[None, :]
        added = jnp.einsum("rb,bis->ris", picker, terms, precision=lax.Precision.HIGHEST)
        flows = lax.dynamic_slice_in_dim(base_flow, area * LINE_DEV, LINE_DEV, 0).astype(jnp.float32)
        post = flows + added.reshape(LINE_DEV, SCEN)
        limit = 0.01 * lax.dynamic_slice_in_dim(rating, area * LINE_DEV, LINE_DEV, 0).astype(jnp.float32)
        weight = lax.dynamic_slice_in_dim(cost, area * LINE_DEV, LINE_DEV, 0)
        excess = jnp.maximum(jnp.abs(post) - limit[:, None], 0.0)
        share = jnp.sum(weight[:, None] * excess * excess, axis=0)
        return carry + share, post.astype(jnp.bfloat16)

    total, posts = lax.scan(one_area, jnp.zeros((SCEN,), jnp.float32), jnp.arange(areas, dtype=jnp.int32))
    return posts.reshape(LINES, SCEN), total / LINES
```

```python
import functools

import jax
import jax.numpy as jnp
from jax import lax
from jax.experimental import pallas as pl
from jax.experimental.pallas import tpu as pltpu
from jax.sharding import PartitionSpec as P

REACH = 6
NEAR = REACH // 2
MESH = pl.DeviceIdType.MESH
ROWS = 512
LAST_ROWS = 256


def kernel(areas, base_hbm, lodf_hbm, row_ref, col_ref, count_ref, outage_ref, rating_ref, cost_ref,
           post_hbm, pen_ref, base, lodf, table, inv_v, inv_s, panels, acc, post, limit, weight,
           shares, in_sem, out_sem, inv_sem, z_send, y_send, core_send, off_recv, core_recv,
           pen_send, pen_recv):
    chips = areas // 2
    small = chips == 8
    line_dev, scen = base.shape
    blk = lodf.shape[1]
    nb = lodf.shape[0] - 1
    rows_blocks = line_dev // blk
    width = 2 * (2 * NEAR + 1)
    here = lax.axis_index("lines")
    core = lax.rem(here, 2)
    chip = here // 2
    partner = chip * 2 + 1 - core

    base_in = pltpu.make_async_copy(base_hbm, base, in_sem.at[0])
    base_in.start()
    lodf_in = pltpu.make_async_copy(lodf_hbm, lodf.at[pl.ds(0, nb)], in_sem.at[1])
    lodf_in.start()

    barrier = pltpu.get_barrier_semaphore()
    if small:
        peers = [lax.rem(here + step, areas) for step in range(1, areas)]
    else:
        peers = [lax.rem(here + 2 * step + areas, areas) for step in range(-NEAR, NEAR + 1) if step != 0]
        peers.append(partner)
    for peer in peers:
        pl.semaphore_signal(barrier, inc=1, device_id={"lines": peer}, device_id_type=MESH)

    def slot(of, at):
        return lax.rem(of - at + NEAR + chips, chips)

    def remote(of, to_chip, to_core, send_sem, recv_sem):
        there = slot(of, to_chip)
        return pltpu.make_async_remote_copy(
            src_ref=panels.at[slot(of, chip), core],
            dst_ref=panels.at[there, core],
            send_sem=send_sem,
            recv_sem=recv_sem.at[there],
            device_id={"lines": to_chip * 2 + to_core},
            device_id_type=MESH,
        )

    def to_core(of):
        return remote(of, chip, 1 - core, core_send.at[slot(of, chip)], core_recv)

    def off_wait(of):
        remote(of, chip, core, y_send.at[0], off_recv).wait_recv()

    picked = jnp.transpose(jnp.broadcast_to(outage_ref[...].astype(jnp.float32), (blk, blk)))
    lane = lax.broadcasted_iota(jnp.int32, (blk, blk), 1)
    ones = jnp.concatenate(
        [(picked == (lane + part * blk).astype(jnp.float32)).astype(jnp.bfloat16) for part in range(rows_blocks)],
        axis=1,
    )
    base_in.wait()
    panels[NEAR, core] = jnp.dot(ones, base[...], preferred_element_type=jnp.float32).astype(jnp.bfloat16)
    pl.semaphore_wait(barrier, len(peers))

    to_core(chip).start()
    if small:
        y = lax.rem(chip, 2)
        z = chip // 2
        across = chip + 1 - 2 * y
        first, last, high = (3 - z) // 3, z // 3, z // 2
        steps = [0, 1 - 2 * last, 3 * first - 1 - last, 2 - 4 * high + first - last]
        signs = [0, 1 - 2 * last, 2 * first - 1, 1 - 2 * high]

        def to_y(of):
            return remote(of, across, core, y_send.at[slot(of, chip)], off_recv)

        def to_z(of, by):
            return remote(of, chip + 2 * by, core, z_send.at[slot(of, chip), (by + 1) // 2], off_recv)

        to_y(chip).start()
        up, down = to_z(chip, 1), to_z(chip, -1)

        @pl.when(z < 3)
        def _():
            up.start()

        @pl.when(z > 0)
        def _():
            down.start()
    else:
        away = [step for step in range(-NEAR, NEAR + 1) if step != 0]

        def direct(step):
            to_chip = lax.rem(chip + step + chips, chips)
            return remote(chip, to_chip, core, y_send.at[step + NEAR], off_recv)

        for step in away:
            direct(step).start()

    offset = lax.rem(col_ref[...] - (2 * chip - REACH) + 2 * areas, areas)
    number = lax.broadcasted_iota(jnp.int32, (1, nb), 1)
    code = jnp.where(number < count_ref[0], row_ref[...] * width + offset, -1)
    pair = lax.broadcasted_iota(jnp.int32, (rows_blocks * width, nb), 0)
    found = jnp.sum(jnp.where(pair == code, number - nb, 0), axis=1, keepdims=True) + nb
    inv_v[...] = jnp.broadcast_to(found, inv_v.shape)
    inv_copy = pltpu.make_async_copy(inv_v, inv_s, inv_sem)
    inv_copy.start()
    lodf[nb] = jnp.zeros((blk, blk), jnp.bfloat16)
    lodf_in.wait()
    inv_copy.wait()

    @pl.loop(0, rows_blocks)
    def _(r):
        for k in range(width):
            at = pl.ds(pl.multiple_of(r * blk, blk), blk)
            table[k // 2, at, (k % 2) * blk:(k % 2 + 1) * blk] = lodf[inv_s[r * width + k, 0]]

    def add(of, start=False):
        m = slot(of, chip)

        @pl.loop(0, line_dev // ROWS)
        def _(i):
            at = pl.ds(pl.multiple_of(i * ROWS, ROWS), ROWS)
            term = jnp.dot(
                table[m, at, :], panels[m].reshape(2 * blk, scen), preferred_element_type=jnp.float32
            )
            acc[at, :] = term if start else acc[at, :] + term

    def core_wait(of):
        to_core(of).wait_recv()

    def spread():
        for r in range(rows_blocks):
            at = slice(r * blk, (r + 1) * blk)
            bound = 0.01 * rating_ref[r:r + 1, :].astype(jnp.float32)
            limit[at, :] = jnp.transpose(jnp.broadcast_to(bound, (blk, blk)))
            weight[at, :] = jnp.transpose(jnp.broadcast_to(cost_ref[r:r + 1, :], (blk, blk)))

    if small:
        def z_event(i):
            of = chip + 2 * steps[i]
            off_wait(of)
            back = z - signs[i]

            @pl.when((back >= 0) & (back <= 3))
            def _():
                to_z(of, -signs[i]).start()

            to_y(of).start()

            @pl.when(steps[i] * signs[i] != 2)
            def _():
                to_core(of).start()

        def y_event(i):
            of = across + 2 * steps[i]
            off_wait(of)
            to_core(of).start()

        def add_z(i):
            @pl.when(steps[i] * signs[i] != 2)
            def _():
                core_wait(chip + 2 * steps[i])
                add(chip + 2 * steps[i])

        def add_y(i):
            core_wait(across + 2 * steps[i])
            add(across + 2 * steps[i])

        core_wait(chip)
        add(chip, True)
        z_event(1)
        y_event(0)
        spread()
        add_y(0)
        z_event(2)
        y_event(1)
        add_z(1)
        add_y(1)
        z_event(3)
        y_event(2)
        add_z(2)
        add_y(2)
        add_z(3)
        y_event(3)
        final = across + 2 * steps[3]
        core_wait(final)
    else:
        core_wait(chip)
        add(chip, True)
        spread()
        near = [1, -1, 2, -2, 3, -3]
        for step in near:
            of = lax.rem(chip + step + chips, chips)
            off_wait(of)
            to_core(of).start()
        for step in near[:-1]:
            of = lax.rem(chip + step + chips, chips)
            core_wait(of)
            add(of)
        final = lax.rem(chip + near[-1] + chips, chips)
        core_wait(final)

    m = slot(final, chip)

    def post_out(i):
        at = pl.ds(pl.multiple_of(i * LAST_ROWS, LAST_ROWS), LAST_ROWS)
        return pltpu.make_async_copy(post.at[at], post_hbm.at[at], out_sem.at[i])

    def last_pass(i, share):
        at = pl.ds(pl.multiple_of(i * LAST_ROWS, LAST_ROWS), LAST_ROWS)
        term = jnp.dot(table[m, at, :], panels[m].reshape(2 * blk, scen), preferred_element_type=jnp.float32)
        flow = base[at, :].astype(jnp.float32) + (acc[at, :] + term)
        post[at, :] = flow.astype(jnp.bfloat16)
        post_out(i).start()
        bound = jnp.concatenate([limit[at, :]] * (scen // blk), axis=1)
        each = jnp.concatenate([weight[at, :]] * (scen // blk), axis=1)
        excess = jnp.maximum(jnp.abs(flow) - bound, 0.0)
        return share + jnp.sum((each * excess * excess).reshape(LAST_ROWS // 8, 8, scen), axis=0)

    passes = line_dev // LAST_ROWS
    share = lax.fori_loop(0, passes, last_pass, jnp.zeros((8, scen), jnp.float32))
    share = jnp.sum(share, axis=0, keepdims=True)

    if small:
        shares[here] = share

        def pen_copy(step):
            other = lax.rem(here + step, areas)
            return pltpu.make_async_remote_copy(
                src_ref=shares.at[here],
                dst_ref=shares.at[here],
                send_sem=pen_send.at[other],
                recv_sem=pen_recv.at[here],
                device_id={"lines": other},
                device_id_type=MESH,
            )

        def pen_wait(step):
            other = lax.rem(here + step, areas)
            return pltpu.make_async_remote_copy(
                src_ref=shares.at[other],
                dst_ref=shares.at[other],
                send_sem=pen_send.at[other],
                recv_sem=pen_recv.at[other],
                device_id={"lines": other},
                device_id_type=MESH,
            )

        for step in range(1, areas):
            pen_copy(step).start()
        to_core(chip).wait_send()
        to_y(chip).wait_send()

        @pl.when(z < 3)
        def _():
            up.wait_send()

        @pl.when(z > 0)
        def _():
            down.wait_send()

        for i in range(4):
            to_core(across + 2 * steps[i]).wait_send()
        for i in range(1, 4):
            of = chip + 2 * steps[i]
            back = z - signs[i]

            @pl.when((back >= 0) & (back <= 3))
            def _():
                to_z(of, -signs[i]).wait_send()

            to_y(of).wait_send()

            @pl.when(steps[i] * signs[i] != 2)
            def _():
                to_core(of).wait_send()

        for i in range(passes):
            post_out(i).wait()
        for step in range(1, areas):
            pen_wait(step).wait_recv()
        total = shares[0]
        for area in range(1, areas):
            total = total + shares[area]
        pen_ref[...] = total / (line_dev * areas)
        for step in range(1, areas):
            pen_copy(step).wait_send()
    else:
        to_core(chip).wait_send()
        for step in away:
            direct(step).wait_send()
            to_core(lax.rem(chip + step + chips, chips)).wait_send()
        for i in range(passes):
            post_out(i).wait()
        pen_ref[...] = share


def on_device(base_flow, lodf_blocks, block_row, block_col, block_count, outage, rating, cost):
    areas = lax.axis_size("lines")
    nb, blk, _ = lodf_blocks.shape
    line_dev, scen = base_flow.shape
    rows_blocks = line_dev // blk
    near = 2 * NEAR + 1
    small = areas == 16
    slots = near + 1
    vmem = pl.BlockSpec(memory_space=pltpu.VMEM)
    smem = pl.BlockSpec(memory_space=pltpu.SMEM)
    anywhere = pl.BlockSpec(memory_space=pl.ANY)
    dma = pltpu.SemaphoreType.DMA
    post, pen = pl.pallas_call(
        functools.partial(kernel, areas),
        out_shape=(
            jax.ShapeDtypeStruct((line_dev, scen), jnp.bfloat16),
            jax.ShapeDtypeStruct((1, scen), jnp.float32),
        ),
        in_specs=[anywhere, anywhere, vmem, vmem, smem, vmem, vmem, vmem],
        out_specs=(anywhere, vmem),
        scratch_shapes=[
            pltpu.VMEM((line_dev, scen), jnp.bfloat16),
            pltpu.VMEM((nb + 1, blk, blk), jnp.bfloat16),
            pltpu.VMEM((near, line_dev, 2 * blk), jnp.bfloat16),
            pltpu.VMEM((rows_blocks * 2 * near, 128), jnp.int32),
            pltpu.SMEM((rows_blocks * 2 * near, 128), jnp.int32),
            pltpu.VMEM((slots, 2, blk, scen), jnp.bfloat16),
            pltpu.VMEM((line_dev, scen), jnp.float32),
            pltpu.VMEM((line_dev, scen), jnp.bfloat16),
            pltpu.VMEM((line_dev, blk), jnp.float32),
            pltpu.VMEM((line_dev, blk), jnp.float32),
            pltpu.VMEM((areas, 1, scen), jnp.float32),
            dma((2,)),
            dma((line_dev // LAST_ROWS,)),
            dma,
            dma((slots, 2)),
            dma((slots,)),
            dma((slots,)),
            dma((slots,)),
            dma((slots,)),
            dma((areas,)),
            dma((areas,)),
        ],
        compiler_params=pltpu.CompilerParams(
            collective_id=0, has_side_effects=True, vmem_limit_bytes=50 * 1024 * 1024
        ),
        cost_estimate=pl.CostEstimate(
            flops=2 * line_dev * 2 * near * blk * scen, bytes_accessed=11000000, transcendentals=0
        ),
    )(
        base_flow,
        lodf_blocks,
        block_row.reshape(1, nb),
        block_col.reshape(1, nb),
        block_count,
        outage.reshape(1, blk),
        rating.reshape(rows_blocks, blk),
        cost.reshape(rows_blocks, blk),
    )
    pen = pen.reshape(scen)
    if not small:
        pen = lax.psum(pen, "lines") / (line_dev * areas)
    return post, pen


def solution(mesh):
    return jax.shard_map(
        on_device,
        mesh=mesh,
        in_specs=(
            P("lines", "groups"),
            P("lines", None, None),
            P("lines"),
            P("lines"),
            P("lines"),
            P("lines"),
            P("lines"),
            P("lines"),
        ),
        out_specs=(P("lines", "groups"), P("groups")),
        check_vma=False,
    )
```

```python
import functools

import jax
import jax.numpy as jnp
from jax import lax
from jax.experimental import pallas as pl
from jax.experimental.pallas import tpu as pltpu
from jax.sharding import PartitionSpec as P

REACH = 6
NEAR = REACH // 2
MESH = pl.DeviceIdType.MESH
ROWS = 512
LAST_ROWS = 256


def kernel(areas, base_hbm, lodf_hbm, row_hbm, col_hbm, count_hbm, outage_hbm, rating_hbm, cost_hbm,
           post_hbm, pen_ref, row_ref, col_ref, count_ref, outage_ref, rating_ref, cost_ref, base, lodf, table, inv_v, inv_s, panels, acc, post, limit, weight,
           shares, in_sem, out_sem, inv_sem, z_send, y_send, core_send, off_recv, core_recv,
           pen_send, pen_recv):
    chips = areas // 2
    small = chips == 8
    line_dev, scen = base.shape
    blk = lodf.shape[1]
    nb = lodf.shape[0] - 1
    rows_blocks = line_dev // blk
    width = 2 * (2 * NEAR + 1)
    here = lax.axis_index("lines")
    core = lax.rem(here, 2)
    chip = here // 2
    partner = chip * 2 + 1 - core

    base_in = pltpu.make_async_copy(base_hbm, base, in_sem.at[0])
    small_in = [
        pltpu.make_async_copy(there, own, in_sem.at[2 + i])
        for i, (there, own) in enumerate([
            (outage_hbm, outage_ref), (row_hbm, row_ref), (col_hbm, col_ref),
            (count_hbm, count_ref), (rating_hbm, rating_ref), (cost_hbm, cost_ref),
        ])
    ]
    small_in[0].start()
    base_in.start()
    for copy in small_in[1:]:
        copy.start()
    lodf_in = pltpu.make_async_copy(lodf_hbm, lodf.at[pl.ds(0, nb)], in_sem.at[1])
    lodf_in.start()

    barrier = pltpu.get_barrier_semaphore()
    if small:
        peers = [lax.rem(here + step, areas) for step in range(1, areas)]
    else:
        peers = [lax.rem(here + 2 * step + areas, areas) for step in range(-NEAR, NEAR + 1) if step != 0]
        peers.append(partner)
    for peer in peers:
        pl.semaphore_signal(barrier, inc=1, device_id={"lines": peer}, device_id_type=MESH)

    def slot(of, at):
        return lax.rem(of - at + NEAR + chips, chips)

    def remote(of, to_chip, to_core, send_sem, recv_sem):
        there = slot(of, to_chip)
        return pltpu.make_async_remote_copy(
            src_ref=panels.at[slot(of, chip), core],
            dst_ref=panels.at[there, core],
            send_sem=send_sem,
            recv_sem=recv_sem.at[there],
            device_id={"lines": to_chip * 2 + to_core},
            device_id_type=MESH,
        )

    def to_core(of):
        return remote(of, chip, 1 - core, core_send.at[slot(of, chip)], core_recv)

    def off_wait(of):
        remote(of, chip, core, y_send.at[0], off_recv).wait_recv()

    small_in[0].wait()
    picked = jnp.transpose(jnp.broadcast_to(outage_ref[...].astype(jnp.float32), (blk, blk)))
    lane = lax.broadcasted_iota(jnp.int32, (blk, blk), 1)
    ones = jnp.concatenate(
        [(picked == (lane + part * blk).astype(jnp.float32)).astype(jnp.bfloat16) for part in range(rows_blocks)],
        axis=1,
    )
    base_in.wait()
    panels[NEAR, core] = jnp.dot(ones, base[...], preferred_element_type=jnp.float32).astype(jnp.bfloat16)
    pl.semaphore_wait(barrier, len(peers))

    if small:
        y = lax.rem(chip, 2)
        z = chip // 2
        across = chip + 1 - 2 * y
        first, last, high = (3 - z) // 3, z // 3, z // 2
        steps = [0, 1 - 2 * last, 3 * first - 1 - last, 2 - 4 * high + first - last]
        signs = [0, 1 - 2 * last, 2 * first - 1, 1 - 2 * high]

        def to_y(of):
            return remote(of, across, core, y_send.at[slot(of, chip)], off_recv)

        def to_z(of, by):
            return remote(of, chip + 2 * by, core, z_send.at[slot(of, chip), (by + 1) // 2], off_recv)

        up, down = to_z(chip, 1), to_z(chip, -1)

        @pl.when(z < 3)
        def _():
            up.start()

        @pl.when(z > 0)
        def _():
            down.start()

        to_y(chip).start()
    else:
        away = [step for step in range(-NEAR, NEAR + 1) if step != 0]

        def direct(step):
            to_chip = lax.rem(chip + step + chips, chips)
            return remote(chip, to_chip, core, y_send.at[step + NEAR], off_recv)

        for step in away:
            direct(step).start()
    to_core(chip).start()

    for copy in small_in[1:]:
        copy.wait()
    offset = lax.rem(col_ref[...] - (2 * chip - REACH) + 2 * areas, areas)
    number = lax.broadcasted_iota(jnp.int32, (1, nb), 1)
    code = jnp.where(number < count_ref[0], row_ref[...] * width + offset, -1)
    pair = lax.broadcasted_iota(jnp.int32, (rows_blocks * width, nb), 0)
    found = jnp.sum(jnp.where(pair == code, number - nb, 0), axis=1, keepdims=True) + nb
    inv_v[...] = jnp.broadcast_to(found, inv_v.shape)
    inv_copy = pltpu.make_async_copy(inv_v, inv_s, inv_sem)
    inv_copy.start()
    lodf[nb] = jnp.zeros((blk, blk), jnp.bfloat16)
    lodf_in.wait()
    inv_copy.wait()

    @pl.loop(0, rows_blocks)
    def _(r):
        for k in range(width):
            at = pl.ds(pl.multiple_of(r * blk, blk), blk)
            table[k // 2, at, (k % 2) * blk:(k % 2 + 1) * blk] = lodf[inv_s[r * width + k, 0]]

    def add(of, start=False):
        m = slot(of, chip)

        @pl.loop(0, line_dev // ROWS)
        def _(i):
            at = pl.ds(pl.multiple_of(i * ROWS, ROWS), ROWS)
            term = jnp.dot(
                table[m, at, :], panels[m].reshape(2 * blk, scen), preferred_element_type=jnp.float32
            )
            acc[at, :] = term if start else acc[at, :] + term

    def core_wait(of):
        to_core(of).wait_recv()

    def spread():
        for r in range(rows_blocks):
            at = slice(r * blk, (r + 1) * blk)
            bound = 0.01 * rating_ref[r:r + 1, :].astype(jnp.float32)
            limit[at, :] = jnp.transpose(jnp.broadcast_to(bound, (blk, blk)))
            weight[at, :] = jnp.transpose(jnp.broadcast_to(cost_ref[r:r + 1, :], (blk, blk)))

    if small:
        def z_event(i):
            of = chip + 2 * steps[i]
            off_wait(of)
            back = z - signs[i]

            @pl.when((back >= 0) & (back <= 3))
            def _():
                to_z(of, -signs[i]).start()

            to_y(of).start()

            @pl.when(steps[i] * signs[i] != 2)
            def _():
                to_core(of).start()

        def y_event(i):
            of = across + 2 * steps[i]
            off_wait(of)
            to_core(of).start()

        def add_z(i):
            @pl.when(steps[i] * signs[i] != 2)
            def _():
                core_wait(chip + 2 * steps[i])
                add(chip + 2 * steps[i])

        def add_y(i):
            core_wait(across + 2 * steps[i])
            add(across + 2 * steps[i])

        core_wait(chip)
        add(chip, True)
        z_event(1)
        y_event(0)
        spread()
        add_y(0)
        z_event(2)
        y_event(1)
        add_z(1)
        add_y(1)
        z_event(3)
        y_event(2)
        add_z(2)
        add_y(2)
        add_z(3)
        y_event(3)
        final = across + 2 * steps[3]
        core_wait(final)
    else:
        core_wait(chip)
        add(chip, True)
        spread()
        near = [1, -1, 2, -2, 3, -3]
        for step in near:
            of = lax.rem(chip + step + chips, chips)
            off_wait(of)
            to_core(of).start()
        for step in near[:-1]:
            of = lax.rem(chip + step + chips, chips)
            core_wait(of)
            add(of)
        final = lax.rem(chip + near[-1] + chips, chips)
        core_wait(final)

    m = slot(final, chip)

    def post_out(i):
        at = pl.ds(pl.multiple_of(i * LAST_ROWS, LAST_ROWS), LAST_ROWS)
        return pltpu.make_async_copy(post.at[at], post_hbm.at[at], out_sem.at[i])

    def last_pass(i, share):
        at = pl.ds(pl.multiple_of(i * LAST_ROWS, LAST_ROWS), LAST_ROWS)
        term = jnp.dot(table[m, at, :], panels[m].reshape(2 * blk, scen), preferred_element_type=jnp.float32)
        flow = base[at, :].astype(jnp.float32) + (acc[at, :] + term)
        post[at, :] = flow.astype(jnp.bfloat16)
        post_out(i).start()
        bound = jnp.concatenate([limit[at, :]] * (scen // blk), axis=1)
        each = jnp.concatenate([weight[at, :]] * (scen // blk), axis=1)
        excess = jnp.maximum(jnp.abs(flow) - bound, 0.0)
        return share + jnp.sum((each * excess * excess).reshape(LAST_ROWS // 8, 8, scen), axis=0)

    passes = line_dev // LAST_ROWS
    share = lax.fori_loop(0, passes, last_pass, jnp.zeros((8, scen), jnp.float32))
    share = jnp.sum(share, axis=0, keepdims=True)

    if small:
        shares[here] = share

        def pen_copy(step):
            other = lax.rem(here + step, areas)
            return pltpu.make_async_remote_copy(
                src_ref=shares.at[here],
                dst_ref=shares.at[here],
                send_sem=pen_send.at[other],
                recv_sem=pen_recv.at[here],
                device_id={"lines": other},
                device_id_type=MESH,
            )

        def pen_wait(step):
            other = lax.rem(here + step, areas)
            return pltpu.make_async_remote_copy(
                src_ref=shares.at[other],
                dst_ref=shares.at[other],
                send_sem=pen_send.at[other],
                recv_sem=pen_recv.at[other],
                device_id={"lines": other},
                device_id_type=MESH,
            )

        for step in range(1, areas):
            pen_copy(step).start()
        to_core(chip).wait_send()
        to_y(chip).wait_send()

        @pl.when(z < 3)
        def _():
            up.wait_send()

        @pl.when(z > 0)
        def _():
            down.wait_send()

        for i in range(4):
            to_core(across + 2 * steps[i]).wait_send()
        for i in range(1, 4):
            of = chip + 2 * steps[i]
            back = z - signs[i]

            @pl.when((back >= 0) & (back <= 3))
            def _():
                to_z(of, -signs[i]).wait_send()

            to_y(of).wait_send()

            @pl.when(steps[i] * signs[i] != 2)
            def _():
                to_core(of).wait_send()

        for i in range(passes):
            post_out(i).wait()
        for step in range(1, areas):
            pen_wait(step).wait_recv()
        total = shares[0]
        for area in range(1, areas):
            total = total + shares[area]
        pen_ref[...] = total / (line_dev * areas)
        for step in range(1, areas):
            pen_copy(step).wait_send()
    else:
        to_core(chip).wait_send()
        for step in away:
            direct(step).wait_send()
            to_core(lax.rem(chip + step + chips, chips)).wait_send()
        for i in range(passes):
            post_out(i).wait()
        pen_ref[...] = share


def on_device(base_flow, lodf_blocks, block_row, block_col, block_count, outage, rating, cost):
    areas = lax.axis_size("lines")
    nb, blk, _ = lodf_blocks.shape
    line_dev, scen = base_flow.shape
    rows_blocks = line_dev // blk
    near = 2 * NEAR + 1
    small = areas == 16
    slots = near + 1
    vmem = pl.BlockSpec(memory_space=pltpu.VMEM)
    in_hbm = pl.BlockSpec(memory_space=pltpu.HBM)
    anywhere = pl.BlockSpec(memory_space=pl.ANY)
    dma = pltpu.SemaphoreType.DMA
    post, pen = pl.pallas_call(
        functools.partial(kernel, areas),
        out_shape=(
            jax.ShapeDtypeStruct((line_dev, scen), jnp.bfloat16),
            jax.ShapeDtypeStruct((1, scen), jnp.float32),
        ),
        in_specs=[in_hbm] * 8,
        out_specs=(anywhere, vmem),
        scratch_shapes=[
            pltpu.VMEM((1, nb), jnp.int32),
            pltpu.VMEM((1, nb), jnp.int32),
            pltpu.SMEM((1,), jnp.int32),
            pltpu.VMEM((1, blk), jnp.int32),
            pltpu.VMEM((rows_blocks, blk), jnp.int32),
            pltpu.VMEM((rows_blocks, blk), jnp.float32),
            pltpu.VMEM((line_dev, scen), jnp.bfloat16),
            pltpu.VMEM((nb + 1, blk, blk), jnp.bfloat16),
            pltpu.VMEM((near, line_dev, 2 * blk), jnp.bfloat16),
            pltpu.VMEM((rows_blocks * 2 * near, 128), jnp.int32),
            pltpu.SMEM((rows_blocks * 2 * near, 128), jnp.int32),
            pltpu.VMEM((slots, 2, blk, scen), jnp.bfloat16),
            pltpu.VMEM((line_dev, scen), jnp.float32),
            pltpu.VMEM((line_dev, scen), jnp.bfloat16),
            pltpu.VMEM((line_dev, blk), jnp.float32),
            pltpu.VMEM((line_dev, blk), jnp.float32),
            pltpu.VMEM((areas, 1, scen), jnp.float32),
            dma((8,)),
            dma((line_dev // LAST_ROWS,)),
            dma,
            dma((slots, 2)),
            dma((slots,)),
            dma((slots,)),
            dma((slots,)),
            dma((slots,)),
            dma((areas,)),
            dma((areas,)),
        ],
        compiler_params=pltpu.CompilerParams(
            collective_id=0, has_side_effects=True, vmem_limit_bytes=63 * 1024 * 1024
        ),
        cost_estimate=pl.CostEstimate(
            flops=2 * line_dev * 2 * near * blk * scen, bytes_accessed=11000000, transcendentals=0
        ),
    )(
        base_flow,
        lodf_blocks,
        block_row.reshape(1, nb),
        block_col.reshape(1, nb),
        block_count,
        outage.reshape(1, blk),
        rating.reshape(rows_blocks, blk),
        cost.reshape(rows_blocks, blk),
    )
    pen = pen.reshape(scen)
    if not small:
        pen = lax.psum(pen, "lines") / (line_dev * areas)
    return post, pen


def solution(mesh):
    return jax.shard_map(
        on_device,
        mesh=mesh,
        in_specs=(
            P("lines", "groups"),
            P("lines", None, None),
            P("lines"),
            P("lines"),
            P("lines"),
            P("lines"),
            P("lines"),
            P("lines"),
        ),
        out_specs=(P("lines", "groups"), P("groups")),
        check_vma=False,
    )
```
